32 devices in a mesh: groups: 2 (over x), row: 8 (over z, y), col: 2 (over core).
Axes of the slice: x: 2, y: 2, z: 4, core: 2. Of those that a mesh axis runs over, the one named last changes fastest.
Arguments:
- voltages: bfloat16 [256, 263936], P(('groups', 'row', 'col')), parts along dimension 0, may hold values from -6 to 6
- owner_block: int32 [16], replicated, may hold values from 0 to 15, each once
Outputs:
- visibility: float32 [32, 8, 2, 128, 128], P(('groups', 'row', 'col')), parts along dimension 0
- beam: float32 [32, 8, 1024], P(('groups', 'row', 'col')), parts along dimension 0
The draws below stay inside these ranges and needn't reach their ends.
There are 2 independent parts, one for each index of `groups`. The reference program is written for one: setup_inputs(seed, part) draws one part's arguments, and reference() takes and returns one part's arrays. A program takes and returns all parts, laid end to end along the dimension named above; an argument that names none is the same for every part. Nothing has to cross between parts.
Inputs may be any that keep to these rules, and one draw needn't show every extreme that they name: owner_block is a permutation: every channel block has exactly one owner device, device d of a part ending with block owner_block[d].
All inputs are finite; a program needn't handle non-finite values.
Results may differ from the reference program's by a relative error of at most 0.0038.
Values may be sent and summed in bfloat16 or wider, within the bound.
No kernel may reach another device: no remote copies, remote signals or barrier semaphores. Data moves between devices by JAX's collectives and lax.ppermute only.
A program may use at most 128 MiB of HBM per device.

```python
import math
import jax
import jax.numpy as jnp
from jax import lax

CHANS = 128
TAPS = 8
IN_DEV = 8
SPECTRA = 1024
NBLK = 16
CH_DEV = 8
INPUTS = 128
SAMPLES = 263936


def level_of(rng, shape, split, low, high):
    def one(dim, parts):
        draws = jax.random.uniform(jax.random.fold_in(jax.random.fold_in(rng, 6), dim), (parts,), jnp.float32, low / len(split), high / len(split))
        return jnp.repeat(jnp.exp(draws), shape[dim] // parts).reshape((-1,) + (1,) * (len(shape) - dim - 1))

    level = one(*split[0])
    for cut in split[1:]:
        level = level * one(*cut)
    return level


def noise(own_key, extent, spread, most, shards=(), held_as=jnp.bfloat16):
    factor_of = level_of(own_key, extent, shards, -0.22, 0.18) if shards else 1.0
    drawn = jax.random.normal(own_key, extent, jnp.float32) * spread * factor_of
    return jnp.minimum(jnp.maximum(drawn, -most), most).astype(held_as)


def setup_inputs(seed: int = 0, part: int = 0) -> dict:
    keys = jax.random.split(jax.random.key(seed), 3)
    own_keys = jax.random.split(jax.random.fold_in(keys[2], part), 3)
    return {
        "voltages": noise(own_keys[0], (INPUTS, SAMPLES), 1.0, 6.0, ((0, 16),)),
        "owner_block": jax.random.permutation(keys[1], NBLK).astype(jnp.int32),
    }


def window_table(tap_count, length):
    total = tap_count * length
    offsets = jnp.arange(total).astype(jnp.float32)
    profile = jnp.sinc((offsets - total / 2 + 0.5) / length) * (0.5 - 0.5 * jnp.cos(2 * math.pi * (offsets + 0.5) / total))
    profile = profile * jnp.sqrt(length / jnp.sum(profile * profile))
    return profile.reshape(tap_count, length).astype(jnp.float32)

def dft_table(channels):
    length = 2 * channels
    times = jnp.arange(length, dtype=jnp.int32)
    freqs = jnp.arange(channels, dtype=jnp.int32)
    steps_mod = freqs[:, None] * times[None, :] % length
    phase = 2 * math.pi * steps_mod.astype(jnp.float32) / length
    table = jnp.concatenate([jnp.cos(phase), -jnp.sin(phase)], 0) / math.sqrt(length)
    return table.astype(jnp.float32).astype(jnp.bfloat16)

def reference(voltages, owner_block):
    length = 2 * CHANS
    window = window_table(TAPS, length)
    fourier = dft_table(CHANS).astype(jnp.float32)
    frames = voltages.reshape(NBLK, IN_DEV, SPECTRA + TAPS - 1, length)

    def channelize(group):
        filtered = jnp.zeros((IN_DEV, SPECTRA, length), jnp.float32)
        for tap_index in range(TAPS):
            filtered = filtered + window[tap_index] * group[:, tap_index:tap_index + SPECTRA, :].astype(jnp.float32)
        filtered = lax.optimization_barrier(filtered.astype(jnp.bfloat16)).astype(jnp.float32)
        spectrum = jnp.einsum('ct,ist->cis', fourier, filtered, precision=lax.Precision.HIGHEST)
        return spectrum.astype(jnp.bfloat16)
    spectra = lax.map(channelize, frames)
    spectra = jnp.moveaxis(spectra, 0, 1).reshape(2, NBLK, CH_DEV, INPUTS, SPECTRA)
    spectra = jnp.moveaxis(spectra, 1, 0)

    def correlate(block):
        real_part = block[0].astype(jnp.float32)
        imag_part = block[1].astype(jnp.float32)
        row_side = jnp.concatenate([real_part, imag_part], axis=2)
        turned = jnp.concatenate([imag_part, -real_part], axis=2)
        stacked = jnp.stack([row_side, turned], 1)
        visibility = jnp.einsum('cpis,cjs->cpij', stacked, row_side, precision=lax.Precision.HIGHEST) / SPECTRA
        beam = lax.optimization_barrier(jnp.sum(real_part * real_part + imag_part * imag_part, axis=1)) / INPUTS
        return (visibility, beam)
    visibility, beam = lax.map(correlate, spectra)
    return (jnp.take(visibility, owner_block, axis=0), jnp.take(beam, owner_block, axis=0))
```

```python
import functools
import math

import jax
import jax.numpy as jnp
import numpy as np
from jax import lax
from jax.experimental import pallas as pl
from jax.experimental.pallas import tpu as pltpu
from jax.sharding import PartitionSpec as P

CHANS = 128
TAPS = 8
SPECTRA = 1024
LENGTH = 2 * CHANS
AXES = ("row", "col")
LANES = 128
FRAME_GROUP = 16
VMEM = 48 * 1024 * 1024


def window_table():
    total = TAPS * LENGTH
    offsets = np.arange(total, dtype=np.float64)
    profile = np.sinc((offsets - total / 2 + 0.5) / LENGTH) * (
        0.5 - 0.5 * np.cos(2 * math.pi * (offsets + 0.5) / total)
    )
    profile = profile * np.sqrt(LENGTH / np.sum(profile * profile))
    return profile.reshape(TAPS, LENGTH).astype(np.float32)


def dft_table():
    times = np.arange(LENGTH)
    freqs = np.arange(CHANS)
    phase = 2 * math.pi * ((freqs[:, None] * times[None, :]) % LENGTH) / LENGTH
    table = np.concatenate([np.cos(phase), -np.sin(phase)], 0) / math.sqrt(LENGTH)
    return table.astype(np.float32).astype(jnp.bfloat16)


def spectra_kernel(tile, in_dev, blocks, owner, frames, window, fourier, *rest):
    outs, (filtered, spectra) = rest[:blocks], rest[blocks:]
    per_block = CHANS // blocks
    me = lax.axis_index(AXES)

    @pl.loop(0, tile // FRAME_GROUP)
    def _(group):
        first = group * FRAME_GROUP
        for half in range(LENGTH // LANES):
            cols = slice(half * LANES, (half + 1) * LANES)
            held = frames[pl.ds(first, FRAME_GROUP + TAPS - 1), :, cols].astype(jnp.float32)
            total = window[0:1, cols] * held[0:FRAME_GROUP]
            for tap in range(1, TAPS):
                total = total + window[tap : tap + 1, cols] * held[tap : tap + FRAME_GROUP]
            filtered[half, pl.ds(first * in_dev, FRAME_GROUP * in_dev), :] = total.reshape(
                FRAME_GROUP * in_dev, LANES
            )

    for i in range(in_dev):
        rows = jnp.concatenate(
            [filtered[half, pl.ds(i, tile, stride=in_dev), :] for half in range(LENGTH // LANES)], axis=1
        ).astype(jnp.bfloat16)
        product = lax.dot_general(
            fourier[...], rows, (((1,), (1,)), ((), ())), preferred_element_type=jnp.float32
        )
        for part in range(tile // LANES):
            spectra[part, pl.ds(i * 2 * CHANS, 2 * CHANS), :] = product[:, part * LANES : (part + 1) * LANES]

    for other in range(blocks):
        base = owner[me ^ other] * per_block
        for channel in range(per_block):
            for part in range(tile // LANES):
                pair = [
                    spectra[part, pl.ds(base + plane * CHANS + channel, in_dev, stride=2 * CHANS), :]
                    for plane in range(2)
                ]
                outs[other][channel, :, part * LANES : (part + 1) * LANES] = jnp.concatenate(
                    pair, axis=0
                ).astype(jnp.bfloat16)


def make_spectra(frames, owner_block, window, fourier, start, count, blocks, tile):
    in_dev = frames.shape[1]
    per_block = CHANS // blocks
    return pl.pallas_call(
        functools.partial(spectra_kernel, tile, in_dev, blocks),
        grid_spec=pltpu.PrefetchScalarGridSpec(
            num_scalar_prefetch=1,
            grid=(count // tile,),
            in_specs=[
                pl.BlockSpec(
                    (pl.Element(tile + TAPS - 1), pl.Element(in_dev), pl.Element(LENGTH)),
                    lambda step, owner: (start + step * tile, 0, 0),
                ),
                pl.BlockSpec((TAPS, LENGTH), lambda step, owner: (0, 0)),
                pl.BlockSpec((LENGTH, LENGTH), lambda step, owner: (0, 0)),
            ],
            out_specs=[
                pl.BlockSpec((per_block, 2 * in_dev, tile), lambda step, owner: (0, 0, step))
                for _ in range(blocks)
            ],
            scratch_shapes=[
                pltpu.VMEM((LENGTH // LANES, tile * in_dev, LANES), jnp.float32),
                pltpu.VMEM((tile // LANES, in_dev * 2 * CHANS, LANES), jnp.float32),
            ],
        ),
        out_shape=[
            jax.ShapeDtypeStruct((per_block, 2 * in_dev, count), jnp.bfloat16) for _ in range(blocks)
        ],
        compiler_params=pltpu.CompilerParams(vmem_limit_bytes=VMEM),
        cost_estimate=pl.CostEstimate(
            flops=2 * count * in_dev * LENGTH * LENGTH, bytes_accessed=4 * count * in_dev * LENGTH, transcendentals=0
        ),
    )(owner_block, frames, window, fourier)


def correlate_kernel(in_dev, blocks, scale, *refs):
    parts, (visibility, beam, planes) = refs[:blocks], refs[blocks:]
    count = parts[0].shape[2]
    inputs = in_dev * blocks
    me = lax.axis_index(AXES)
    channel = pl.program_id(0)
    power = jnp.zeros((in_dev, count), jnp.float32)
    for other in range(blocks):
        wide = parts[other][0].astype(jnp.float32)
        real_part, imag_part = wide[:in_dev], wide[in_dev:]
        power = power + (real_part * real_part + imag_part * imag_part)
        source = me ^ other
        planes[0, source] = real_part
        planes[1, source] = imag_part
    beam[pl.ds(channel, 1), :] = jnp.sum(power, axis=0, keepdims=True) * (1.0 / inputs)
    both = planes[...].reshape(2 * inputs, count).astype(jnp.bfloat16)
    gram = lax.dot_general(both, both, (((1,), (1,)), ((), ())), preferred_element_type=jnp.float32)
    visibility[0, 0] = (gram[:inputs, :inputs] + gram[inputs:, inputs:]) * scale
    visibility[0, 1] = (gram[inputs:, :inputs] - gram[:inputs, inputs:]) * scale


def correlate(parts, blocks):
    per_block, rows, count = parts[0].shape
    in_dev = rows // 2
    inputs = in_dev * blocks
    return pl.pallas_call(
        functools.partial(correlate_kernel, in_dev, blocks, 1.0 / SPECTRA),
        grid=(per_block,),
        in_specs=[pl.BlockSpec((1, rows, count), lambda channel: (channel, 0, 0)) for _ in range(blocks)],
        out_specs=[
            pl.BlockSpec((1, 2, inputs, inputs), lambda channel: (channel, 0, 0, 0)),
            pl.BlockSpec((per_block, count), lambda channel: (0, 0)),
        ],
        scratch_shapes=[pltpu.VMEM((2, blocks, in_dev, count), jnp.float32)],
        out_shape=[
            jax.ShapeDtypeStruct((per_block, 2, inputs, inputs), jnp.float32),
            jax.ShapeDtypeStruct((per_block, count), jnp.float32),
        ],
        compiler_params=pltpu.CompilerParams(vmem_limit_bytes=VMEM),
        cost_estimate=pl.CostEstimate(
            flops=8 * per_block * inputs * inputs * count, bytes_accessed=4 * per_block * inputs * count, transcendentals=0
        ),
    )(*parts)


def body(voltages, owner_block):
    in_dev = voltages.shape[0]
    blocks = lax.axis_size(AXES)
    window = jnp.asarray(window_table())
    fourier = jnp.asarray(dft_table())
    frames = voltages.reshape(in_dev, SPECTRA + TAPS - 1, LENGTH).transpose(1, 0, 2)
    own = make_spectra(frames, owner_block, window, fourier, 0, SPECTRA, blocks, 256)
    parts = [own[0]] + [
        lax.ppermute(own[other], AXES, [(source, source ^ other) for source in range(blocks)])
        for other in range(1, blocks)
    ]
    visibility, beam = correlate(parts, blocks)
    return (visibility[None], beam[None])


def solution(mesh):
    in_specs = (P(("groups", "row", "col"), None), P())
    out_specs = (
        P(("groups", "row", "col"), None, None, None, None),
        P(("groups", "row", "col"), None, None),
    )
    return jax.shard_map(body, mesh=mesh, in_specs=in_specs, out_specs=out_specs, check_vma=False)
```

```python
import functools
import math

import jax
import jax.numpy as jnp
import numpy as np
from jax import lax
from jax.experimental import pallas as pl
from jax.experimental.pallas import tpu as pltpu
from jax.sharding import PartitionSpec as P

CHANS = 128
TAPS = 8
SPECTRA = 1024
LENGTH = 2 * CHANS
AXES = ("row", "col")
LANES = 128
FRAME_GROUP = 16
VMEM = 48 * 1024 * 1024


def window_table():
    total = TAPS * LENGTH
    offsets = np.arange(total, dtype=np.float64)
    profile = np.sinc((offsets - total / 2 + 0.5) / LENGTH) * (
        0.5 - 0.5 * np.cos(2 * math.pi * (offsets + 0.5) / total)
    )
    profile = profile * np.sqrt(LENGTH / np.sum(profile * profile))
    return profile.reshape(TAPS, LENGTH).astype(np.float32)


def dft_table():
    times = np.arange(LENGTH)
    freqs = np.arange(CHANS)
    phase = 2 * math.pi * ((freqs[:, None] * times[None, :]) % LENGTH) / LENGTH
    table = np.concatenate([np.cos(phase), -np.sin(phase)], 0) / math.sqrt(LENGTH)
    return table.astype(np.float32).astype(jnp.bfloat16)


def spectra_kernel(tile, in_dev, blocks, others, held_back, owner, frames, window, fourier, *rest):
    outs, (filtered, spectra) = rest[held_back:-2], rest[-2:]
    per_block = CHANS // blocks
    me = lax.axis_index(AXES)

    @pl.loop(0, tile // FRAME_GROUP)
    def _(group):
        first = group * FRAME_GROUP
        for half in range(LENGTH // LANES):
            cols = slice(half * LANES, (half + 1) * LANES)
            held = frames[pl.ds(first, FRAME_GROUP + TAPS - 1), :, cols].astype(jnp.float32)
            total = window[0:1, cols] * held[0:FRAME_GROUP]
            for tap in range(1, TAPS):
                total = total + window[tap : tap + 1, cols] * held[tap : tap + FRAME_GROUP]
            filtered[half, pl.ds(first * in_dev, FRAME_GROUP * in_dev), :] = total.reshape(
                FRAME_GROUP * in_dev, LANES
            )

    for i in range(in_dev):
        rows = jnp.concatenate(
            [filtered[half, pl.ds(i, tile, stride=in_dev), :] for half in range(LENGTH // LANES)], axis=1
        ).astype(jnp.bfloat16)
        product = lax.dot_general(
            fourier[...], rows, (((1,), (1,)), ((), ())), preferred_element_type=jnp.float32
        )
        for part in range(tile // LANES):
            spectra[part, pl.ds(i * 2 * CHANS, 2 * CHANS), :] = product[:, part * LANES : (part + 1) * LANES]

    for other, out in zip(others, outs):
        base = owner[me ^ other] * per_block
        for channel in range(per_block):
            for part in range(tile // LANES):
                pair = [
                    spectra[part, pl.ds(base + plane * CHANS + channel, in_dev, stride=2 * CHANS), :]
                    for plane in range(2)
                ]
                out[channel, :, part * LANES : (part + 1) * LANES] = jnp.concatenate(
                    pair, axis=0
                ).astype(jnp.bfloat16)


def make_spectra(tables, frames, owner_block, start, count, blocks, fresh, whole, kept=(), tile=256):
    in_dev = frames.shape[1]
    per_block = CHANS // blocks
    rows = 2 * in_dev
    return pl.pallas_call(
        functools.partial(spectra_kernel, tile, in_dev, blocks, fresh + whole, len(kept)),
        grid_spec=pltpu.PrefetchScalarGridSpec(
            num_scalar_prefetch=1,
            grid=(count // tile,),
            in_specs=[
                pl.BlockSpec(
                    (pl.Element(tile + TAPS - 1), pl.Element(in_dev), pl.Element(LENGTH)),
                    lambda step, owner: (start + step * tile, 0, 0),
                ),
                pl.BlockSpec((TAPS, LENGTH), lambda step, owner: (0, 0)),
                pl.BlockSpec((LENGTH, LENGTH), lambda step, owner: (0, 0)),
            ]
            + [pl.BlockSpec(memory_space=pl.ANY) for _ in kept],
            out_specs=[pl.BlockSpec((per_block, rows, tile), lambda step, owner: (0, 0, step)) for _ in fresh]
            + [
                pl.BlockSpec((per_block, rows, tile), lambda step, owner: (0, 0, start // tile + step))
                for _ in whole
            ],
            scratch_shapes=[
                pltpu.VMEM((LENGTH // LANES, tile * in_dev, LANES), jnp.float32),
                pltpu.VMEM((tile // LANES, in_dev * 2 * CHANS, LANES), jnp.float32),
            ],
        ),
        out_shape=[jax.ShapeDtypeStruct((per_block, rows, count), jnp.bfloat16) for _ in fresh]
        + [jax.ShapeDtypeStruct((per_block, rows, SPECTRA), jnp.bfloat16) for _ in whole],
        input_output_aliases={4 + index: len(fresh) + index for index in range(len(kept))},
        compiler_params=pltpu.CompilerParams(vmem_limit_bytes=VMEM),
        cost_estimate=pl.CostEstimate(
            flops=2 * count * in_dev * LENGTH * LENGTH, bytes_accessed=4 * count * in_dev * LENGTH, transcendentals=0
        ),
    )(owner_block, frames, *tables, *kept)


def correlate_kernel(in_dev, blocks, scale, held_back, *refs):
    parts, (visibility, beam, planes) = refs[:blocks], refs[-3:]
    count = parts[0].shape[2]
    inputs = in_dev * blocks
    me = lax.axis_index(AXES)
    channel = pl.program_id(0)
    power = jnp.zeros((in_dev, count), jnp.float32)
    for other in range(blocks):
        wide = parts[other][0].astype(jnp.float32)
        real_part, imag_part = wide[:in_dev], wide[in_dev:]
        power = power + (real_part * real_part + imag_part * imag_part)
        source = me ^ other
        planes[0, source] = real_part
        planes[1, source] = imag_part
    beam[pl.ds(channel, 1), :] = jnp.sum(power, axis=0, keepdims=True) * (1.0 / inputs)
    both = planes[...].reshape(2 * inputs, count).astype(jnp.bfloat16)
    gram = lax.dot_general(both, both, (((1,), (1,)), ((), ())), preferred_element_type=jnp.float32)
    straight = (gram[:inputs, :inputs] + gram[inputs:, inputs:]) * scale
    crossed = (gram[inputs:, :inputs] - gram[:inputs, inputs:]) * scale
    if held_back:
        before = refs[blocks]
        straight = before[0, 0] + straight
        crossed = before[0, 1] + crossed
    visibility[0, 0] = straight
    visibility[0, 1] = crossed


def correlate(parts, start, count, blocks, kept=()):
    per_block, rows, _ = parts[0].shape
    in_dev = rows // 2
    inputs = in_dev * blocks

    def part_spec(part):
        place = start // count if part.shape[2] == SPECTRA else 0
        return pl.BlockSpec((1, rows, count), lambda channel: (channel, 0, place))

    visibility_spec = pl.BlockSpec((1, 2, inputs, inputs), lambda channel: (channel, 0, 0, 0))
    return pl.pallas_call(
        functools.partial(correlate_kernel, in_dev, blocks, 1.0 / SPECTRA, len(kept)),
        grid=(per_block,),
        in_specs=[part_spec(part) for part in parts]
        + ([visibility_spec, pl.BlockSpec(memory_space=pl.ANY)] if kept else []),
        out_specs=[visibility_spec, pl.BlockSpec((per_block, count), lambda channel: (0, start // count))],
        scratch_shapes=[pltpu.VMEM((2, blocks, in_dev, count), jnp.float32)],
        out_shape=[
            jax.ShapeDtypeStruct((per_block, 2, inputs, inputs), jnp.float32),
            jax.ShapeDtypeStruct((per_block, SPECTRA), jnp.float32),
        ],
        input_output_aliases={blocks: 0, blocks + 1: 1} if kept else {},
        compiler_params=pltpu.CompilerParams(vmem_limit_bytes=VMEM),
        cost_estimate=pl.CostEstimate(
            flops=8 * per_block * inputs * inputs * count, bytes_accessed=4 * per_block * inputs * count, transcendentals=0
        ),
    )(*parts, *kept)


FIRST, MIDDLE, LAST = (768, 256), (0, 512), (512, 256)
IN_FLIGHT = 5


def body(voltages, owner_block):
    in_dev = voltages.shape[0]
    blocks = lax.axis_size(AXES)
    tables = (jnp.asarray(window_table()), jnp.asarray(dft_table()))
    frames = voltages.reshape(in_dev, SPECTRA + TAPS - 1, LENGTH).transpose(1, 0, 2)
    far, near = tuple(range(blocks // 2, blocks)), tuple(range(blocks // 2))
    spectra = functools.partial(make_spectra, tables, frames, owner_block, blocks=blocks)

    sent, taken = [], {}

    def send(name, other, block):
        if len(sent) >= IN_FLIGHT:
            block, taken[sent[-IN_FLIGHT]] = lax.optimization_barrier((block, taken[sent[-IN_FLIGHT]]))
        taken[name, other] = lax.ppermute(block, AXES, [(s, s ^ other) for s in range(blocks)])
        sent.append((name, other))

    made = spectra(*FIRST, fresh=far, whole=near)
    first, kept = made[: len(far)], made[len(far) :]
    for other, block in zip(far, first):
        send("first", other, block)
    made = spectra(*MIDDLE, fresh=far, whole=near, kept=kept)
    middle, kept = made[: len(far)], made[len(far) :]
    made = spectra(*LAST, fresh=far, whole=near, kept=kept)
    last, kept = made[: len(far)], made[len(far) :]
    taken["near", 0] = kept[0]
    for index, other in enumerate(far):
        send("middle", other, middle[index])
        if index + 1 < len(near):
            send("near", near[index + 1], kept[index + 1])
    for other, block in zip(far, last):
        send("last", other, block)
    result = ()
    for name, chunk in (("first", FIRST), ("middle", MIDDLE), ("last", LAST)):
        parts = [taken["near", other] for other in near] + [taken[name, other] for other in far]
        result = correlate(parts, *chunk, blocks, result)
    visibility, beam = result
    return (visibility[None], beam[None])


def solution(mesh):
    in_specs = (P(("groups", "row", "col"), None), P())
    out_specs = (
        P(("groups", "row", "col"), None, None, None, None),
        P(("groups", "row", "col"), None, None),
    )
    return jax.shard_map(body, mesh=mesh, in_specs=in_specs, out_specs=out_specs, check_vma=False)
```

```python
import functools
import math

import jax
import jax.numpy as jnp
import numpy as np
from jax import lax
from jax.experimental import pallas as pl
from jax.experimental.pallas import tpu as pltpu
from jax.sharding import PartitionSpec as P

CHANS = 128
TAPS = 8
SPECTRA = 1024
LENGTH = 2 * CHANS
AXES = ("row", "col")
LANES = 128
FRAME_GROUP = 16
TILE = 128
VMEM = 40 * 1024 * 1024


def window_table():
    total = TAPS * LENGTH
    offsets = np.arange(total, dtype=np.float64)
    profile = np.sinc((offsets - total / 2 + 0.5) / LENGTH) * (
        0.5 - 0.5 * np.cos(2 * math.pi * (offsets + 0.5) / total)
    )
    profile = profile * np.sqrt(LENGTH / np.sum(profile * profile))
    return profile.reshape(TAPS, LENGTH).astype(np.float32)


def dft_table():
    times = np.arange(LENGTH)
    freqs = np.arange(CHANS)
    phase = 2 * math.pi * ((freqs[:, None] * times[None, :]) % LENGTH) / LENGTH
    table = np.concatenate([np.cos(phase), -np.sin(phase)], 0) / math.sqrt(LENGTH)
    return table.astype(np.float32).astype(jnp.bfloat16)


def spectra_tile(start, first_row, in_dev, targets, base_of, outs, frames, window, fourier, filtered, spectra):
    @pl.loop(0, TILE // FRAME_GROUP)
    def _(group):
        first = start + group * FRAME_GROUP
        for half in range(LENGTH // LANES):
            cols = slice(half * LANES, (half + 1) * LANES)
            held = frames[pl.ds(first, FRAME_GROUP + TAPS - 1), :, cols].astype(jnp.float32)
            total = window[0:1, cols] * held[0:FRAME_GROUP]
            for tap in range(1, TAPS):
                total = total + window[tap : tap + 1, cols] * held[tap : tap + FRAME_GROUP]
            filtered[half, pl.ds(group * FRAME_GROUP * in_dev, FRAME_GROUP * in_dev), :] = total.reshape(
                FRAME_GROUP * in_dev, LANES
            )

    first_row()
    for i in range(in_dev):
        rows = jnp.concatenate(
            [filtered[half, pl.ds(i, TILE, stride=in_dev), :] for half in range(LENGTH // LANES)], axis=1
        ).astype(jnp.bfloat16)
        product = lax.dot_general(
            fourier[...], rows, (((1,), (1,)), ((), ())), preferred_element_type=jnp.float32
        )
        for part in range(TILE // LANES):
            spectra[part, pl.ds(i * 2 * CHANS, 2 * CHANS), :] = product[:, part * LANES : (part + 1) * LANES]
    for (other, low, width), out in zip(targets, outs):
        if not low <= start < low + width:
            continue
        base = base_of(other)
        offset = start - low
        for channel in range(out.shape[0]):
            for part in range(TILE // LANES):
                pair = [
                    spectra[part, pl.ds(base + plane * CHANS + channel, in_dev, stride=2 * CHANS), :]
                    for plane in range(2)
                ]
                out[channel, :, offset + part * LANES : offset + (part + 1) * LANES] = jnp.concatenate(
                    pair, axis=0
                ).astype(jnp.bfloat16)


def first_spectra_kernel(count, in_dev, blocks, targets, *refs):
    owner_in, frames_in, window_in, fourier_in = refs[:4]
    outs = refs[4 : 4 + len(targets)]
    frames, window, fourier, owner_held, filtered, spectra, owner, arrived = refs[4 + len(targets) :]
    me = lax.axis_index(AXES)
    needed, total = count + TAPS - 1, SPECTRA + TAPS - 1
    window_copy = pltpu.make_async_copy(window_in, window, arrived.at[0])
    fourier_copy = pltpu.make_async_copy(fourier_in, fourier, arrived.at[1])
    owner_copy = pltpu.make_async_copy(owner_in, owner, arrived.at[2])
    held_copy = pltpu.make_async_copy(owner_in, owner_held, arrived.at[3])
    edges = [0, TILE + TAPS - 1, needed, total]
    frame_copies = [
        pltpu.make_async_copy(frames_in.at[pl.ds(low, high - low)], frames.at[pl.ds(low, high - low)], arrived.at[4 + index])
        for index, (low, high) in enumerate(zip(edges, edges[1:]))
    ]
    copies = [window_copy, frame_copies[0], fourier_copy, owner_copy, *frame_copies[1:], held_copy]
    for copy in copies:
        copy.start()
    window_copy.wait()
    for start in range(0, count, TILE):
        if start < 2 * TILE:
            frame_copies[start // TILE].wait()

        def tables_here():
            if start == 0:
                fourier_copy.wait()
                owner_copy.wait()

        spectra_tile(
            start, tables_here, in_dev, targets, lambda other: owner[me ^ other] * (CHANS // blocks),
            outs, frames, window, fourier, filtered, spectra,
        )
    held_copy.wait()
    frame_copies[2].wait()


def spectra_kernel(first, count, in_dev, blocks, targets, kept, *refs):
    frames, window, fourier, owner_held = refs[:4]
    outs = refs[4 + kept : 4 + kept + len(targets)]
    filtered, spectra, owner, arrived = refs[4 + kept + len(targets) :]
    me = lax.axis_index(AXES)
    owner_copy = pltpu.make_async_copy(owner_held, owner, arrived.at[0])
    owner_copy.start()
    owner_copy.wait()
    for start in range(first, first + count, TILE):
        spectra_tile(
            start, lambda: None, in_dev, targets, lambda other: owner[me ^ other] * (CHANS // blocks),
            outs, frames, window, fourier, filtered, spectra,
        )


def make_spectra(inputs, start, count, in_dev, blocks, targets, kept=()):
    per_block = CHANS // blocks
    rows = 2 * in_dev
    vmem, hbm = pl.BlockSpec(memory_space=pltpu.VMEM), pl.BlockSpec(memory_space=pltpu.HBM)
    out_shape = [jax.ShapeDtypeStruct((per_block, rows, width), jnp.bfloat16) for _, _, width in targets]
    scratch = [
        pltpu.VMEM((LENGTH // LANES, TILE * in_dev, LANES), jnp.float32),
        pltpu.VMEM((TILE // LANES, in_dev * 2 * CHANS, LANES), jnp.float32),
        pltpu.SMEM((blocks,), jnp.int32),
    ]
    if start == 0:
        owner_block, frames, window, fourier = inputs
        kernel = functools.partial(first_spectra_kernel, count, in_dev, blocks, targets)
        out_shape += [jax.ShapeDtypeStruct(x.shape, x.dtype) for x in (frames, window, fourier, owner_block)]
        in_specs = [hbm] * 4
        inputs = [pltpu.with_memory_space_constraint(x, pltpu.HBM) for x in inputs]
        scratch.append(pltpu.SemaphoreType.DMA((7,)))
    else:
        kernel = functools.partial(spectra_kernel, start, count, in_dev, blocks, targets, len(kept))
        in_specs = [vmem] * (4 + len(kept))
        scratch.append(pltpu.SemaphoreType.DMA((1,)))
    return pl.pallas_call(
        kernel,
        in_specs=in_specs,
        out_specs=[vmem] * len(out_shape),
        out_shape=out_shape,
        scratch_shapes=scratch,
        input_output_aliases={4 + index: len(targets) - len(kept) + index for index in range(len(kept))},
        compiler_params=pltpu.CompilerParams(vmem_limit_bytes=VMEM),
    )(*inputs, *kept)


def correlate_kernel(in_dev, blocks, start, count, chunks, *refs):
    parts = refs[:blocks]
    per_block = parts[0].shape[0]
    inputs = in_dev * blocks
    me = lax.axis_index(AXES)
    if chunks:
        before, beams = refs[blocks], refs[blocks + 1 : blocks + 1 + len(chunks)]
        visibility_out, beam_out, visibility, beam, left = refs[blocks + 1 + len(chunks) : blocks + 6 + len(chunks)]
        planes = refs[blocks + 6 + len(chunks) :]
        copies = [
            pltpu.make_async_copy(held, beam_out.at[:, pl.ds(first, size)], left.at[per_block + 1 + index])
            for index, ((first, size), held) in enumerate(zip(chunks, beams))
        ]
        for copy in copies:
            copy.start()
    else:
        before = refs[blocks] if len(refs) == blocks + 3 + per_block else None
        visibility, beam = refs[-per_block - 2 : -per_block]
        planes = refs[-per_block:]
    for channel in range(per_block):
        power = jnp.zeros((in_dev, count), jnp.float32)
        for other in range(blocks):
            place = start if parts[other].shape[2] == SPECTRA else 0
            wide = parts[other][channel, :, place : place + count].astype(jnp.float32)
            real_part, imag_part = wide[:in_dev], wide[in_dev:]
            power = power + (real_part * real_part + imag_part * imag_part)
            source = me ^ other
            planes[channel][0, source] = real_part
            planes[channel][1, source] = imag_part
        beam[channel : channel + 1, :] = jnp.sum(power, axis=0, keepdims=True) * (1.0 / inputs)
        both = planes[channel][...].reshape(2 * inputs, count).astype(jnp.bfloat16)
        gram = lax.dot_general(both, both, (((1,), (1,)), ((), ())), preferred_element_type=jnp.float32)
        straight = (gram[:inputs, :inputs] + gram[inputs:, inputs:]) * (1.0 / SPECTRA)
        crossed = (gram[inputs:, :inputs] - gram[:inputs, inputs:]) * (1.0 / SPECTRA)
        if before is not None:
            straight = before[channel, 0] + straight
            crossed = before[channel, 1] + crossed
        visibility[channel, 0] = straight
        visibility[channel, 1] = crossed
        if chunks:
            copies.append(
                pltpu.make_async_copy(visibility.at[channel], visibility_out.at[channel], left.at[channel])
            )
            copies[-1].start()
    if chunks:
        copies.append(pltpu.make_async_copy(beam, beam_out.at[:, pl.ds(start, count)], left.at[per_block]))
        copies[-1].start()
        for copy in copies:
            copy.wait()


def correlate(parts, start, count, blocks, before=None, chunks=(), beams=()):
    per_block, rows, _ = parts[0].shape
    in_dev = rows // 2
    inputs = in_dev * blocks
    visibility = (per_block, 2, inputs, inputs)
    space = pltpu.HBM if chunks else pltpu.VMEM
    staged = [
        pltpu.VMEM(visibility, jnp.float32),
        pltpu.VMEM((per_block, count), jnp.float32),
        pltpu.SemaphoreType.DMA((per_block + 1 + len(chunks),)),
    ]
    operands = [*parts, *([] if before is None else [before]), *beams]
    return pl.pallas_call(
        functools.partial(correlate_kernel, in_dev, blocks, start, count, chunks),
        in_specs=[pl.BlockSpec(memory_space=pltpu.VMEM)] * len(operands),
        out_specs=[pl.BlockSpec(memory_space=space)] * 2,
        scratch_shapes=(staged if chunks else [])
        + [pltpu.VMEM((2, blocks, in_dev, count), jnp.float32) for _ in range(per_block)],
        out_shape=[
            jax.ShapeDtypeStruct(visibility, jnp.float32),
            jax.ShapeDtypeStruct((per_block, SPECTRA if chunks else count), jnp.float32),
        ],
        compiler_params=pltpu.CompilerParams(vmem_limit_bytes=VMEM),
    )(*operands)


FAR_CHUNKS = ((0, 384), (384, 384), (768, 256))
FIRST_FRAMES = 384
IN_FLIGHT = 5


def body(voltages, owner_block):
    in_dev = voltages.shape[0]
    blocks = lax.axis_size(AXES)
    frames = voltages.reshape(in_dev, SPECTRA + TAPS - 1, LENGTH).transpose(1, 0, 2)
    inputs = (owner_block, frames, jnp.asarray(window_table()), jnp.asarray(dft_table()))
    far, near = tuple(range(blocks // 2, blocks)), tuple(range(blocks // 2))
    sent, taken = [], {}

    def after(value, key):
        value, taken[key] = lax.optimization_barrier((value, taken[key]))
        return value

    def send(name, other, block):
        if len(sent) >= IN_FLIGHT:
            block = after(block, sent[-IN_FLIGHT])
        taken[name, other] = lax.ppermute(block, AXES, [(s, s ^ other) for s in range(blocks)])
        sent.append((name, other))

    outgoing = {}
    near_targets = [(other, 0, SPECTRA) for other in near]
    chunks = [c for c in FAR_CHUNKS if c[0] < FIRST_FRAMES]
    targets = [(other, *chunk) for chunk in chunks for other in far] + near_targets
    made = make_spectra(inputs, 0, FIRST_FRAMES, in_dev, blocks, targets)
    inputs, kept = made[len(targets) :], made[len(targets) - len(near) : len(targets)]
    outgoing.update(((low, other), block) for (other, low, _), block in zip(targets, made))
    for low, _ in chunks:
        for other in far:
            send(low, other, outgoing[low, other])
    chunks = [c for c in FAR_CHUNKS if c[0] >= FIRST_FRAMES]
    targets = [(other, *chunk) for chunk in chunks for other in far] + near_targets
    made = make_spectra(inputs, FIRST_FRAMES, SPECTRA - FIRST_FRAMES, in_dev, blocks, targets, kept)
    outgoing.update(((low, other), block) for (other, low, _), block in zip(targets, made))
    taken["near", 0] = outgoing[0, 0]
    others = list(near[1:])
    for low, _ in chunks:
        for other in far:
            send(low, other, outgoing[low, other])
            if others:
                send("near", others[0], outgoing[0, others.pop(0)])

    visibility, beams = None, ()
    for index, (low, count) in enumerate(FAR_CHUNKS):
        parts = [taken["near", other] for other in near] + [taken[low, other] for other in far]
        done = FAR_CHUNKS[:index] if index + 1 == len(FAR_CHUNKS) else ()
        visibility, beam = correlate(parts, low, count, blocks, visibility, done, beams if done else ())
        beams += (beam,)
    return (visibility[None], beam[None])


def solution(mesh):
    in_specs = (P(("groups", "row", "col"), None), P())
    out_specs = (
        P(("groups", "row", "col"), None, None, None, None),
        P(("groups", "row", "col"), None, None),
    )
    return jax.shard_map(body, mesh=mesh, in_specs=in_specs, out_specs=out_specs, check_vma=False)
```

```python
import functools
import math

import jax
import jax.numpy as jnp
import numpy as np
from jax import lax
from jax.experimental import pallas as pl
from jax.experimental.pallas import tpu as pltpu
from jax.sharding import PartitionSpec as P

CHANS = 128
TAPS = 8
SPECTRA = 1024
LENGTH = 2 * CHANS
AXES = ("row", "col")
LANES = 128
FRAME_GROUP = 16
TILE = 128
VMEM = 40 * 1024 * 1024


def window_table():
    total = TAPS * LENGTH
    offsets = np.arange(total, dtype=np.float64)
    profile = np.sinc((offsets - total / 2 + 0.5) / LENGTH) * (
        0.5 - 0.5 * np.cos(2 * math.pi * (offsets + 0.5) / total)
    )
    profile = profile * np.sqrt(LENGTH / np.sum(profile * profile))
    return profile.reshape(TAPS, LENGTH).astype(np.float32)


def dft_table():
    times = np.arange(LENGTH)
    freqs = np.arange(CHANS)
    phase = 2 * math.pi * ((freqs[:, None] * times[None, :]) % LENGTH) / LENGTH
    table = np.concatenate([np.cos(phase), -np.sin(phase)], 0) / math.sqrt(LENGTH)
    return table.astype(np.float32).astype(jnp.bfloat16)


def spectra_tile(start, first_row, in_dev, targets, base_of, outs, frames, window, fourier, filtered, spectra):
    @pl.loop(0, TILE // FRAME_GROUP)
    def _(group):
        first = start + group * FRAME_GROUP
        for half in range(LENGTH // LANES):
            cols = slice(half * LANES, (half + 1) * LANES)
            held = frames[pl.ds(first, FRAME_GROUP + TAPS - 1), :, cols].astype(jnp.float32)
            total = window[0:1, cols] * held[0:FRAME_GROUP]
            for tap in range(1, TAPS):
                total = total + window[tap : tap + 1, cols] * held[tap : tap + FRAME_GROUP]
            filtered[half, pl.ds(group * FRAME_GROUP * in_dev, FRAME_GROUP * in_dev), :] = total.reshape(
                FRAME_GROUP * in_dev, LANES
            )

    first_row()
    for i in range(in_dev):
        rows = jnp.concatenate(
            [filtered[half, pl.ds(i, TILE, stride=in_dev), :] for half in range(LENGTH // LANES)], axis=1
        ).astype(jnp.bfloat16)
        product = lax.dot_general(
            fourier[...], rows, (((1,), (1,)), ((), ())), preferred_element_type=jnp.float32
        )
        for part in range(TILE // LANES):
            spectra[part, pl.ds(i * 2 * CHANS, 2 * CHANS), :] = product[:, part * LANES : (part + 1) * LANES]
    for (other, low, width), out in zip(targets, outs):
        if not low <= start < low + width:
            continue
        base = base_of(other)
        offset = start - low
        for channel in range(out.shape[0]):
            for part in range(TILE // LANES):
                pair = [
                    spectra[part, pl.ds(base + plane * CHANS + channel, in_dev, stride=2 * CHANS), :]
                    for plane in range(2)
                ]
                out[channel, :, offset + part * LANES : offset + (part + 1) * LANES] = jnp.concatenate(
                    pair, axis=0
                ).astype(jnp.bfloat16)


def first_spectra_kernel(count, in_dev, blocks, targets, *refs):
    owner_in, frames_in, window_in, fourier_in = refs[:4]
    per_block = CHANS // blocks
    outs = [refs[4].at[pl.ds(index * per_block, per_block)] for index in range(len(targets))]
    frames, window, fourier, owner_held, filtered, spectra, owner, arrived = refs[5:]
    me = lax.axis_index(AXES)
    needed, total = count + TAPS - 1, SPECTRA + TAPS - 1
    window_copy = pltpu.make_async_copy(window_in, window, arrived.at[0])
    fourier_copy = pltpu.make_async_copy(fourier_in, fourier, arrived.at[1])
    owner_copy = pltpu.make_async_copy(owner_in, owner, arrived.at[2])
    held_copy = pltpu.make_async_copy(owner_in, owner_held, arrived.at[3])
    edges = sorted({0, TILE + TAPS - 1, needed, total})
    frame_copies = [
        pltpu.make_async_copy(frames_in.at[pl.ds(low, high - low)], frames.at[pl.ds(low, high - low)], arrived.at[4 + index])
        for index, (low, high) in enumerate(zip(edges, edges[1:]))
    ]
    copies = [window_copy, frame_copies[0], fourier_copy, owner_copy, *frame_copies[1:], held_copy]
    for copy in copies:
        copy.start()
    window_copy.wait()
    for start in range(0, count, TILE):
        if start < 2 * TILE:
            frame_copies[start // TILE].wait()

        def tables_here():
            if start == 0:
                fourier_copy.wait()
                owner_copy.wait()

        spectra_tile(
            start, tables_here, in_dev, targets, lambda other: owner[me ^ other] * (CHANS // blocks),
            outs, frames, window, fourier, filtered, spectra,
        )
    held_copy.wait()
    frame_copies[-1].wait()


def spectra_kernel(count, in_dev, blocks, targets, *refs):
    frames, window, fourier, owner_held = refs[:4]
    outs = refs[4 : 4 + len(targets)]
    filtered, spectra, owner, arrived = refs[4 + len(targets) :]
    me = lax.axis_index(AXES)
    owner_copy = pltpu.make_async_copy(owner_held, owner, arrived.at[0])
    owner_copy.start()
    owner_copy.wait()
    for start in range(0, count, TILE):
        spectra_tile(
            start, lambda: None, in_dev, targets, lambda other: owner[me ^ other] * (CHANS // blocks),
            outs, frames, window, fourier, filtered, spectra,
        )


def make_spectra(inputs, count, in_dev, blocks, targets, first):
    per_block = CHANS // blocks
    rows = 2 * in_dev
    vmem, hbm = pl.BlockSpec(memory_space=pltpu.VMEM), pl.BlockSpec(memory_space=pltpu.HBM)
    out_shape = [jax.ShapeDtypeStruct((per_block, rows, width), jnp.bfloat16) for _, _, width in targets]
    scratch = [
        pltpu.VMEM((LENGTH // LANES, TILE * in_dev, LANES), jnp.float32),
        pltpu.VMEM((TILE // LANES, in_dev * 2 * CHANS, LANES), jnp.float32),
        pltpu.SMEM((blocks,), jnp.int32),
    ]
    if first:
        owner_block, frames, window, fourier = inputs
        kernel = functools.partial(first_spectra_kernel, count, in_dev, blocks, targets)
        out_shape = [jax.ShapeDtypeStruct((len(targets) * per_block, rows, count), jnp.bfloat16)]
        out_shape += [jax.ShapeDtypeStruct(x.shape, x.dtype) for x in (frames, window, fourier, owner_block)]
        in_specs = [hbm] * 4
        inputs = [pltpu.with_memory_space_constraint(x, pltpu.HBM) for x in inputs]
        scratch.append(pltpu.SemaphoreType.DMA((7,)))
    else:
        kernel = functools.partial(spectra_kernel, count, in_dev, blocks, targets)
        in_specs = [vmem] * 4
        scratch.append(pltpu.SemaphoreType.DMA((1,)))
    return pl.pallas_call(
        kernel,
        in_specs=in_specs,
        out_specs=[vmem] * len(out_shape),
        out_shape=out_shape,
        scratch_shapes=scratch,
        compiler_params=pltpu.CompilerParams(vmem_limit_bytes=VMEM),
    )(*inputs)


def correlate_kernel(in_dev, blocks, start, count, chunks, *refs):
    parts = refs[:blocks]
    per_block = parts[0].shape[0]
    inputs = in_dev * blocks
    me = lax.axis_index(AXES)
    if chunks:
        before, beams = refs[blocks], refs[blocks + 1 : blocks + 1 + len(chunks)]
        visibility_out, beam_out, visibility, beam, left = refs[blocks + 1 + len(chunks) : blocks + 6 + len(chunks)]
        planes = refs[blocks + 6 + len(chunks) :]
        copies = [
            pltpu.make_async_copy(held, beam_out.at[:, pl.ds(first, size)], left.at[per_block + 1 + index])
            for index, ((first, size), held) in enumerate(zip(chunks, beams))
        ]
        for copy in copies:
            copy.start()
    else:
        before = refs[blocks] if len(refs) == blocks + 3 + per_block else None
        visibility, beam = refs[-per_block - 2 : -per_block]
        planes = refs[-per_block:]
    for channel in range(per_block):
        power = jnp.zeros((in_dev, count), jnp.float32)
        for other in range(blocks):
            place = start if parts[other].shape[2] == SPECTRA else 0
            wide = parts[other][channel, :, place : place + count].astype(jnp.float32)
            real_part, imag_part = wide[:in_dev], wide[in_dev:]
            power = power + (real_part * real_part + imag_part * imag_part)
            source = me ^ other
            planes[channel][0, source] = real_part
            planes[channel][1, source] = imag_part
        beam[channel : channel + 1, :] = jnp.sum(power, axis=0, keepdims=True) * (1.0 / inputs)
        both = planes[channel][...].reshape(2 * inputs, count).astype(jnp.bfloat16)
        gram = lax.dot_general(both, both, (((1,), (1,)), ((), ())), preferred_element_type=jnp.float32)
        straight = (gram[:inputs, :inputs] + gram[inputs:, inputs:]) * (1.0 / SPECTRA)
        crossed = (gram[inputs:, :inputs] - gram[:inputs, inputs:]) * (1.0 / SPECTRA)
        if before is not None:
            straight = before[channel, 0] + straight
            crossed = before[channel, 1] + crossed
        visibility[channel, 0] = straight
        visibility[channel, 1] = crossed
        if chunks:
            copies.append(
                pltpu.make_async_copy(visibility.at[channel], visibility_out.at[channel], left.at[channel])
            )
            copies[-1].start()
    if chunks:
        copies.append(pltpu.make_async_copy(beam, beam_out.at[:, pl.ds(start, count)], left.at[per_block]))
        copies[-1].start()
        for copy in copies:
            copy.wait()


def correlate(parts, start, count, blocks, before=None, chunks=(), beams=()):
    per_block, rows, _ = parts[0].shape
    in_dev = rows // 2
    inputs = in_dev * blocks
    visibility = (per_block, 2, inputs, inputs)
    space = pltpu.HBM if chunks else pltpu.VMEM
    staged = [
        pltpu.VMEM(visibility, jnp.float32),
        pltpu.VMEM((per_block, count), jnp.float32),
        pltpu.SemaphoreType.DMA((per_block + 1 + len(chunks),)),
    ]
    operands = [*parts, *([] if before is None else [before]), *beams]
    return pl.pallas_call(
        functools.partial(correlate_kernel, in_dev, blocks, start, count, chunks),
        in_specs=[pl.BlockSpec(memory_space=pltpu.VMEM)] * len(operands),
        out_specs=[pl.BlockSpec(memory_space=space)] * 2,
        scratch_shapes=(staged if chunks else [])
        + [pltpu.VMEM((2, blocks, in_dev, count), jnp.float32) for _ in range(per_block)],
        out_shape=[
            jax.ShapeDtypeStruct(visibility, jnp.float32),
            jax.ShapeDtypeStruct((per_block, SPECTRA if chunks else count), jnp.float32),
        ],
        compiler_params=pltpu.CompilerParams(vmem_limit_bytes=VMEM),
    )(*operands)


LEAD = 4
LEAD_FRAMES = 384
IN_FLIGHT = 5


def body(voltages, owner_block):
    in_dev = voltages.shape[0]
    blocks = lax.axis_size(AXES)
    half, per_block = blocks // 2, CHANS // blocks
    frames = voltages.reshape(in_dev, SPECTRA + TAPS - 1, LENGTH).transpose(1, 0, 2)
    inputs = (owner_block, frames, jnp.asarray(window_table()), jnp.asarray(dft_table()))
    far, near = tuple(range(half, blocks)), tuple(range(half))
    sent, taken = [], {}

    def send(target, block, other):
        if len(sent) >= IN_FLIGHT:
            before = sent[-IN_FLIGHT]
            block, taken[before] = lax.optimization_barrier((block, taken[before]))
        taken[target] = lax.ppermute(block, AXES, [(s, s ^ other) for s in range(blocks)])
        sent.append(target)

    first = [(other, 0, LEAD_FRAMES) for other in far[:LEAD]]
    made = make_spectra(inputs, LEAD_FRAMES, in_dev, blocks, first, True)
    send(first[0], made[0], half)
    last = [(other, LEAD_FRAMES, SPECTRA - LEAD_FRAMES) for other in far[:LEAD]]
    across = [(other, 0, SPECTRA) for other in far[LEAD:]]
    close = [(other, 0, SPECTRA) for other in near]
    targets = across + last + close
    ready = dict(zip(targets, make_spectra(made[1:], SPECTRA, in_dev, blocks, targets, False)))
    taken[close[0]] = ready[close[0]]
    distant, others = across + last, close[1:]
    handed = first[1:]
    for index, target in enumerate(distant):
        send(target, ready[target], target[0])
        if index < len(others):
            send(others[index], ready[others[index]], others[index][0])
        if index >= 1 and index - 1 < len(handed):
            offset = index * per_block
            send(handed[index - 1], taken[first[0]][offset : offset + per_block], handed[index - 1][0] - half)

    visibility, beam = correlate([taken[target] for target in close + first + across], 0, LEAD_FRAMES, blocks)
    visibility, beam = correlate(
        [taken[target] for target in close + last + across], LEAD_FRAMES, SPECTRA - LEAD_FRAMES, blocks,
        visibility, ((0, LEAD_FRAMES),), (beam,),
    )
    return (visibility[None], beam[None])


def solution(mesh):
    in_specs = (P(("groups", "row", "col"), None), P())
    out_specs = (
        P(("groups", "row", "col"), None, None, None, None),
        P(("groups", "row", "col"), None, None),
    )
    return jax.shard_map(body, mesh=mesh, in_specs=in_specs, out_specs=out_specs, check_vma=False)
```

```python
import functools
import math

import jax
import jax.numpy as jnp
import numpy as np
from jax import lax
from jax.experimental import pallas as pl
from jax.experimental.pallas import tpu as pltpu
from jax.sharding import PartitionSpec as P

CHANS = 128
TAPS = 8
SPECTRA = 1024
LENGTH = 2 * CHANS
AXES = ("row", "col")
LANES = 128
FRAME_GROUP = 16
TILE = 256
VMEM = 40 * 1024 * 1024


def window_table():
    total = TAPS * LENGTH
    offsets = np.arange(total, dtype=np.float64)
    profile = np.sinc((offsets - total / 2 + 0.5) / LENGTH) * (
        0.5 - 0.5 * np.cos(2 * math.pi * (offsets + 0.5) / total)
    )
    profile = profile * np.sqrt(LENGTH / np.sum(profile * profile))
    return profile.reshape(TAPS, LENGTH).astype(np.float32)


def dft_table():
    times = np.arange(LENGTH)
    freqs = np.arange(CHANS)
    phase = 2 * math.pi * ((freqs[:, None] * times[None, :]) % LENGTH) / LENGTH
    table = np.concatenate([np.cos(phase), -np.sin(phase)], 0) / math.sqrt(LENGTH)
    return table.astype(np.float32).astype(jnp.bfloat16)


def spectra_tile(start, first_row, in_dev, targets, base_of, outs, frames, window, fourier, filtered, spectra):
    @pl.loop(0, TILE // FRAME_GROUP)
    def _(group):
        first = start + group * FRAME_GROUP
        for half in range(LENGTH // LANES):
            cols = slice(half * LANES, (half + 1) * LANES)
            held = frames[pl.ds(first, FRAME_GROUP + TAPS - 1), :, cols].astype(jnp.float32)
            total = window[0:1, cols] * held[0:FRAME_GROUP]
            for tap in range(1, TAPS):
                total = total + window[tap : tap + 1, cols] * held[tap : tap + FRAME_GROUP]
            filtered[half, pl.ds(group * FRAME_GROUP * in_dev, FRAME_GROUP * in_dev), :] = total.reshape(
                FRAME_GROUP * in_dev, LANES
            )

    first_row()
    for i in range(in_dev):
        rows = jnp.concatenate(
            [filtered[half, pl.ds(i, TILE, stride=in_dev), :] for half in range(LENGTH // LANES)], axis=1
        ).astype(jnp.bfloat16)
        product = lax.dot_general(
            fourier[...], rows, (((1,), (1,)), ((), ())), preferred_element_type=jnp.float32
        )
        for part in range(TILE // LANES):
            spectra[part, pl.ds(i * 2 * CHANS, 2 * CHANS), :] = product[:, part * LANES : (part + 1) * LANES]
    for (other, low, width), out in zip(targets, outs):
        if not low <= start < low + width:
            continue
        base = base_of(other)
        offset = start - low
        for channel in range(out.shape[0]):
            for part in range(TILE // LANES):
                pair = [
                    spectra[part, pl.ds(base + plane * CHANS + channel, in_dev, stride=2 * CHANS), :]
                    for plane in range(2)
                ]
                out[channel, :, offset + part * LANES : offset + (part + 1) * LANES] = jnp.concatenate(
                    pair, axis=0
                ).astype(jnp.bfloat16)


def first_spectra_kernel(count, in_dev, blocks, targets, *refs):
    owner_in, frames_in, window_in, fourier_in = refs[:4]
    per_block = CHANS // blocks
    outs = [refs[4].at[pl.ds(index * per_block, per_block)] for index in range(len(targets))]
    frames, window, fourier, owner_held, filtered, spectra, owner, arrived = refs[5:]
    me = lax.axis_index(AXES)
    needed, total = count + TAPS - 1, SPECTRA + TAPS - 1
    window_copy = pltpu.make_async_copy(window_in, window, arrived.at[0])
    fourier_copy = pltpu.make_async_copy(fourier_in, fourier, arrived.at[1])
    owner_copy = pltpu.make_async_copy(owner_in, owner, arrived.at[2])
    held_copy = pltpu.make_async_copy(owner_in, owner_held, arrived.at[3])
    edges = sorted({0, TILE + TAPS - 1, needed, total})
    frame_copies = [
        pltpu.make_async_copy(frames_in.at[pl.ds(low, high - low)], frames.at[pl.ds(low, high - low)], arrived.at[4 + index])
        for index, (low, high) in enumerate(zip(edges, edges[1:]))
    ]
    copies = [window_copy, frame_copies[0], fourier_copy, owner_copy, *frame_copies[1:], held_copy]
    for copy in copies:
        copy.start()
    window_copy.wait()
    for start in range(0, count, TILE):
        if start < 2 * TILE:
            frame_copies[start // TILE].wait()

        def tables_here():
            if start == 0:
                fourier_copy.wait()
                owner_copy.wait()

        spectra_tile(
            start, tables_here, in_dev, targets, lambda other: owner[me ^ other] * (CHANS // blocks),
            outs, frames, window, fourier, filtered, spectra,
        )
    held_copy.wait()
    frame_copies[-1].wait()


def spectra_kernel(count, in_dev, blocks, targets, *refs):
    frames, window, fourier, owner_held = refs[:4]
    outs = refs[4 : 4 + len(targets)]
    filtered, spectra, owner, arrived = refs[4 + len(targets) :]
    me = lax.axis_index(AXES)
    owner_copy = pltpu.make_async_copy(owner_held, owner, arrived.at[0])
    owner_copy.start()
    owner_copy.wait()
    for start in range(0, count, TILE):
        spectra_tile(
            start, lambda: None, in_dev, targets, lambda other: owner[me ^ other] * (CHANS // blocks),
            outs, frames, window, fourier, filtered, spectra,
        )


def make_spectra(inputs, count, in_dev, blocks, targets, first):
    per_block = CHANS // blocks
    rows = 2 * in_dev
    vmem, hbm = pl.BlockSpec(memory_space=pltpu.VMEM), pl.BlockSpec(memory_space=pltpu.HBM)
    out_shape = [jax.ShapeDtypeStruct((per_block, rows, width), jnp.bfloat16) for _, _, width in targets]
    scratch = [
        pltpu.VMEM((LENGTH // LANES, TILE * in_dev, LANES), jnp.float32),
        pltpu.VMEM((TILE // LANES, in_dev * 2 * CHANS, LANES), jnp.float32),
        pltpu.SMEM((blocks,), jnp.int32),
    ]
    if first:
        owner_block, frames, window, fourier = inputs
        kernel = functools.partial(first_spectra_kernel, count, in_dev, blocks, targets)
        out_shape = [jax.ShapeDtypeStruct((len(targets) * per_block, rows, count), jnp.bfloat16)]
        out_shape += [jax.ShapeDtypeStruct(x.shape, x.dtype) for x in (frames, window, fourier, owner_block)]
        in_specs = [hbm] * 4
        inputs = [pltpu.with_memory_space_constraint(x, pltpu.HBM) for x in inputs]
        scratch.append(pltpu.SemaphoreType.DMA((7,)))
    else:
        kernel = functools.partial(spectra_kernel, count, in_dev, blocks, targets)
        in_specs = [vmem] * 4
        scratch.append(pltpu.SemaphoreType.DMA((1,)))
    return pl.pallas_call(
        kernel,
        in_specs=in_specs,
        out_specs=[vmem] * len(out_shape),
        out_shape=out_shape,
        scratch_shapes=scratch,
        compiler_params=pltpu.CompilerParams(vmem_limit_bytes=VMEM),
    )(*inputs)


def correlate_kernel(in_dev, blocks, places, start, count, chunks, *refs):
    parts = refs[:blocks]
    per_block = parts[0].shape[0]
    inputs = in_dev * blocks
    me = lax.axis_index(AXES)
    if chunks:
        before, beams = refs[blocks], refs[blocks + 1 : blocks + 1 + len(chunks)]
        visibility_out, beam_out, visibility, beam, left = refs[blocks + 1 + len(chunks) : blocks + 6 + len(chunks)]
        planes = refs[blocks + 6 + len(chunks) :]
        copies = [
            pltpu.make_async_copy(held, beam_out.at[:, pl.ds(first, size)], left.at[per_block + 1 + index])
            for index, ((first, size), held) in enumerate(zip(chunks, beams))
        ]
        for copy in copies:
            copy.start()
    else:
        before = refs[blocks] if len(refs) == blocks + 3 + per_block else None
        visibility, beam = refs[-per_block - 2 : -per_block]
        planes = refs[-per_block:]
    for channel in range(per_block):
        power = jnp.zeros((in_dev, count), jnp.float32)
        for other in range(blocks):
            wide = parts[other][channel, :, places[other] : places[other] + count].astype(jnp.float32)
            real_part, imag_part = wide[:in_dev], wide[in_dev:]
            power = power + (real_part * real_part + imag_part * imag_part)
            source = me ^ other
            planes[channel][0, source] = real_part
            planes[channel][1, source] = imag_part
        beam[channel : channel + 1, :] = jnp.sum(power, axis=0, keepdims=True) * (1.0 / inputs)
        both = planes[channel][...].reshape(2 * inputs, count).astype(jnp.bfloat16)
        gram = lax.dot_general(both, both, (((1,), (1,)), ((), ())), preferred_element_type=jnp.float32)
        straight = (gram[:inputs, :inputs] + gram[inputs:, inputs:]) * (1.0 / SPECTRA)
        crossed = (gram[inputs:, :inputs] - gram[:inputs, inputs:]) * (1.0 / SPECTRA)
        if before is not None:
            straight = before[channel, 0] + straight
            crossed = before[channel, 1] + crossed
        visibility[channel, 0] = straight
        visibility[channel, 1] = crossed
        if chunks:
            copies.append(
                pltpu.make_async_copy(visibility.at[channel], visibility_out.at[channel], left.at[channel])
            )
            copies[-1].start()
    if chunks:
        copies.append(pltpu.make_async_copy(beam, beam_out.at[:, pl.ds(start, count)], left.at[per_block]))
        copies[-1].start()
        for copy in copies:
            copy.wait()


def correlate(parts, start, count, blocks, before=None, chunks=(), beams=()):
    parts, places = zip(*parts)
    per_block, rows, _ = parts[0].shape
    in_dev = rows // 2
    inputs = in_dev * blocks
    visibility = (per_block, 2, inputs, inputs)
    space = pltpu.HBM if chunks else pltpu.VMEM
    staged = [
        pltpu.VMEM(visibility, jnp.float32),
        pltpu.VMEM((per_block, count), jnp.float32),
        pltpu.SemaphoreType.DMA((per_block + 1 + len(chunks),)),
    ]
    operands = [*parts, *([] if before is None else [before]), *beams]
    return pl.pallas_call(
        functools.partial(correlate_kernel, in_dev, blocks, places, start, count, chunks),
        in_specs=[pl.BlockSpec(memory_space=pltpu.VMEM)] * len(operands),
        out_specs=[pl.BlockSpec(memory_space=space)] * 2,
        scratch_shapes=(staged if chunks else [])
        + [pltpu.VMEM((2, blocks, in_dev, count), jnp.float32) for _ in range(per_block)],
        out_shape=[
            jax.ShapeDtypeStruct(visibility, jnp.float32),
            jax.ShapeDtypeStruct((per_block, SPECTRA if chunks else count), jnp.float32),
        ],
        compiler_params=pltpu.CompilerParams(vmem_limit_bytes=VMEM),
    )(*operands)


LEAD = 6
LEAD_FRAMES = 256
NEAR_ORDER = (4,5,1,2,6,3,7)
NEARS_AHEAD = (0, 1, 1, 1, 2, 1, 1, 0)
IN_FLIGHT = 5


def body(voltages, owner_block):
    in_dev = voltages.shape[0]
    blocks = lax.axis_size(AXES)
    half, per_block = blocks // 2, CHANS // blocks
    frames = voltages.reshape(in_dev, SPECTRA + TAPS - 1, LENGTH).transpose(1, 0, 2)
    inputs = (owner_block, frames, jnp.asarray(window_table()), jnp.asarray(dft_table()))
    far, near = tuple(range(half, blocks)), tuple(range(half))
    sent, taken = [], {}

    def send(target, block, other):
        if len(sent) >= IN_FLIGHT:
            before = sent[: 1 - IN_FLIGHT]
            block, *held = lax.optimization_barrier((block, *(taken[key] for key in before)))
            taken.update(zip(before, held))
        taken[target] = lax.ppermute(block, AXES, [(s, s ^ other) for s in range(blocks)])
        sent.append(target)

    first = [(other, 0, LEAD_FRAMES) for other in far[:LEAD]]
    made = make_spectra(inputs, LEAD_FRAMES, in_dev, blocks, first, True)
    send(first[0], made[0], half)
    last = [(other, LEAD_FRAMES, SPECTRA - LEAD_FRAMES) for other in far[:LEAD]]
    across = [(other, 0, SPECTRA) for other in far[LEAD:]]
    close = [(other, 0, SPECTRA) for other in near]
    targets = across + last + close
    ready = dict(zip(targets, make_spectra(made[1:], SPECTRA, in_dev, blocks, targets, False)))
    taken[close[0]] = ready[close[0]]
    distant, others = list(across + last), [close[step] for step in NEAR_ORDER if step < half]
    others += [target for target in close[1:] if target not in others]
    order = []
    for near_before in NEARS_AHEAD:
        order += others[:near_before] + distant[:1]
        others, distant = others[near_before:], distant[1:]
    for target in order + others + distant:
        block, step = ready[target], target[0]
        if 0 < step < LEAD:
            handed = taken[first[0]][step * per_block : (step + 1) * per_block]
            block = jnp.concatenate([block, handed], axis=2)
        send(target, block, step)

    places = {first[0]: (taken[first[0]], 0)}
    places.update((first[step], (taken[close[step]], SPECTRA)) for step in range(1, LEAD))
    early = [(taken[target], 0) for target in close] + [places[target] for target in first]
    late = [(taken[target], LEAD_FRAMES) for target in close] + [(taken[target], 0) for target in last]
    visibility, beam = correlate(early + [(taken[target], 0) for target in across], 0, LEAD_FRAMES, blocks)
    visibility, beam = correlate(
        late + [(taken[target], LEAD_FRAMES) for target in across], LEAD_FRAMES, SPECTRA - LEAD_FRAMES, blocks,
        visibility, ((0, LEAD_FRAMES),), (beam,),
    )
    return (visibility[None], beam[None])


def solution(mesh):
    in_specs = (P(("groups", "row", "col"), None), P())
    out_specs = (
        P(("groups", "row", "col"), None, None, None, None),
        P(("groups", "row", "col"), None, None),
    )
    return jax.shard_map(body, mesh=mesh, in_specs=in_specs, out_specs=out_specs, check_vma=False)
```

```python
import functools
import math

import jax
import jax.numpy as jnp
import numpy as np
from jax import lax
from jax.experimental import pallas as pl
from jax.experimental.pallas import tpu as pltpu
from jax.sharding import PartitionSpec as P

CHANS = 128
TAPS = 8
SPECTRA = 1024
LENGTH = 2 * CHANS
AXES = ("row", "col")
LANES = 128
FRAME_GROUP = 16
FIRST_TILE = 128
TILE = 256
VMEM = 40 * 1024 * 1024


def window_table():
    total = TAPS * LENGTH
    offsets = np.arange(total, dtype=np.float64)
    profile = np.sinc((offsets - total / 2 + 0.5) / LENGTH) * (
        0.5 - 0.5 * np.cos(2 * math.pi * (offsets + 0.5) / total)
    )
    profile = profile * np.sqrt(LENGTH / np.sum(profile * profile))
    return profile.reshape(TAPS, LENGTH).astype(np.float32)


def dft_table():
    times = np.arange(LENGTH)
    freqs = np.arange(CHANS)
    phase = 2 * math.pi * ((freqs[:, None] * times[None, :]) % LENGTH) / LENGTH
    table = np.concatenate([np.cos(phase), -np.sin(phase)], 0) / math.sqrt(LENGTH)
    return table.astype(np.float32).astype(jnp.bfloat16).astype(np.float32)


def spectra_tile(start, in_dev, targets, base_of, outs, frames, window, fourier, filtered, spectra):
    tile = filtered.shape[1] // in_dev

    @pl.loop(0, tile // FRAME_GROUP)
    def _(group):
        first = start + group * FRAME_GROUP
        for half in range(LENGTH // LANES):
            cols = slice(half * LANES, (half + 1) * LANES)
            held = frames[pl.ds(first, FRAME_GROUP + TAPS - 1), :, cols].astype(jnp.float32)
            total = window[0:1, cols] * held[0:FRAME_GROUP]
            for tap in range(1, TAPS):
                total = total + window[tap : tap + 1, cols] * held[tap : tap + FRAME_GROUP]
            filtered[half, pl.ds(group * FRAME_GROUP * in_dev, FRAME_GROUP * in_dev), :] = total.reshape(
                FRAME_GROUP * in_dev, LANES
            )

    table = fourier()
    height = table.shape[0]
    for i in range(in_dev):
        rows = jnp.concatenate(
            [filtered[half, pl.ds(i, tile, stride=in_dev), :] for half in range(LENGTH // LANES)], axis=1
        ).astype(jnp.bfloat16)
        product = lax.dot_general(
            table, rows, (((1,), (1,)), ((), ())), preferred_element_type=jnp.float32
        )
        for part in range(tile // LANES):
            spectra[part, pl.ds(i * height, height), :] = product[:, part * LANES : (part + 1) * LANES]
    for (other, low, width), out in zip(targets, outs):
        if not low <= start < low + width:
            continue
        bases = base_of(other)
        offset = start - low
        for channel in range(out.shape[0]):
            for part in range(tile // LANES):
                pair = [
                    spectra[part, pl.ds(base + channel, in_dev, stride=height), :]
                    for base in bases
                ]
                out[channel, :, offset + part * LANES : offset + (part + 1) * LANES] = jnp.concatenate(
                    pair, axis=0
                ).astype(jnp.bfloat16)


def first_spectra_kernel(count, in_dev, blocks, targets, *refs):
    owner_in, frames_in, window_in, fourier_in = refs[:4]
    per_block = CHANS // blocks
    outs = [refs[4].at[pl.ds(index * per_block, per_block)] for index in range(len(targets))]
    frames, window, fourier, owner_held, filtered, spectra, owner, arrived = refs[5:]
    me = lax.axis_index(AXES)
    aligned, order = per_block % 8 == 0, [other for other, _, _ in targets]
    needed, total = count + TAPS - 1, SPECTRA + TAPS - 1
    window_copy = pltpu.make_async_copy(window_in, window, arrived.at[0])
    fourier_copy = pltpu.make_async_copy(fourier_in, fourier, arrived.at[1])
    owner_copy = pltpu.make_async_copy(owner_in, owner, arrived.at[2])
    held_copy = pltpu.make_async_copy(owner_in, owner_held, arrived.at[3])
    edges = sorted({0, FIRST_TILE + TAPS - 1, needed, total})
    frame_copies = [
        pltpu.make_async_copy(frames_in.at[pl.ds(low, high - low)], frames.at[pl.ds(low, high - low)], arrived.at[4 + index])
        for index, (low, high) in enumerate(zip(edges, edges[1:]))
    ]
    copies = [window_copy, frame_copies[0], fourier_copy, owner_copy, *frame_copies[1:], held_copy]
    for copy in copies:
        copy.start()
    window_copy.wait()
    for start in range(0, count, FIRST_TILE):
        if start < 2 * FIRST_TILE:
            frame_copies[start // FIRST_TILE].wait()

        def needed_rows():
            if start == 0:
                fourier_copy.wait()
                owner_copy.wait()
            if not aligned:
                return fourier[...].astype(jnp.bfloat16)
            return jnp.concatenate(
                [
                    fourier[pl.ds(pl.multiple_of(owner[me ^ other] * per_block + plane * CHANS, per_block), per_block), :]
                    for other, _, _ in targets
                    for plane in range(2)
                ],
                axis=0,
            ).astype(jnp.bfloat16)

        def base_of(other):
            if aligned:
                index = order.index(other)
                return 2 * index * per_block, (2 * index + 1) * per_block
            return tuple(owner[me ^ other] * per_block + plane * CHANS for plane in range(2))

        spectra_tile(start, in_dev, targets, base_of, outs, frames, window, needed_rows, filtered, spectra)
    held_copy.wait()
    frame_copies[-1].wait()


def spectra_kernel(count, in_dev, blocks, targets, *refs):
    frames, window, fourier, owner_held = refs[:4]
    outs = refs[4 : 4 + len(targets)]
    filtered, spectra, owner, arrived = refs[4 + len(targets) :]
    me = lax.axis_index(AXES)
    owner_copy = pltpu.make_async_copy(owner_held, owner, arrived.at[0])
    owner_copy.start()
    owner_copy.wait()

    def base_of(other):
        return tuple(owner[me ^ other] * (CHANS // blocks) + plane * CHANS for plane in range(2))

    for start in range(0, count, TILE):
        spectra_tile(
            start, in_dev, targets, base_of, outs, frames, window, lambda: fourier[...].astype(jnp.bfloat16), filtered, spectra
        )


def make_spectra(inputs, count, in_dev, blocks, targets, first):
    per_block = CHANS // blocks
    rows = 2 * in_dev
    vmem, hbm = pl.BlockSpec(memory_space=pltpu.VMEM), pl.BlockSpec(memory_space=pltpu.HBM)
    out_shape = [jax.ShapeDtypeStruct((per_block, rows, width), jnp.bfloat16) for _, _, width in targets]
    tile = FIRST_TILE if first else TILE
    scratch = [
        pltpu.VMEM((LENGTH // LANES, tile * in_dev, LANES), jnp.float32),
        pltpu.VMEM((tile // LANES, in_dev * 2 * CHANS, LANES), jnp.float32),
        pltpu.SMEM((blocks,), jnp.int32),
    ]
    if first:
        owner_block, frames, window, fourier = inputs
        kernel = functools.partial(first_spectra_kernel, count, in_dev, blocks, targets)
        out_shape = [jax.ShapeDtypeStruct((len(targets) * per_block, rows, count), jnp.bfloat16)]
        out_shape += [jax.ShapeDtypeStruct(x.shape, x.dtype) for x in (frames, window, fourier, owner_block)]
        in_specs = [hbm] * 4
        inputs = [pltpu.with_memory_space_constraint(x, pltpu.HBM) for x in inputs]
        scratch.append(pltpu.SemaphoreType.DMA((8,)))
    else:
        kernel = functools.partial(spectra_kernel, count, in_dev, blocks, targets)
        in_specs = [vmem] * 4
        scratch.append(pltpu.SemaphoreType.DMA((1,)))
    return pl.pallas_call(
        kernel,
        in_specs=in_specs,
        out_specs=[vmem] * len(out_shape),
        out_shape=out_shape,
        scratch_shapes=scratch,
        compiler_params=pltpu.CompilerParams(vmem_limit_bytes=VMEM),
    )(*inputs)


def correlate_kernel(in_dev, blocks, places, start, count, chunks, *refs):
    parts = refs[:blocks]
    per_block = parts[0].shape[0]
    inputs = in_dev * blocks
    me = lax.axis_index(AXES)
    if chunks:
        before, beams = refs[blocks], refs[blocks + 1 : blocks + 1 + len(chunks)]
        visibility_out, beam_out, visibility, beam, left = refs[blocks + 1 + len(chunks) : blocks + 6 + len(chunks)]
        planes = refs[blocks + 6 + len(chunks) :]
        copies = [
            pltpu.make_async_copy(held, beam_out.at[:, pl.ds(first, size)], left.at[per_block + 1 + index])
            for index, ((first, size), held) in enumerate(zip(chunks, beams))
        ]
        for copy in copies:
            copy.start()
    else:
        before = refs[blocks] if len(refs) == blocks + 3 + per_block else None
        visibility, beam = refs[-per_block - 2 : -per_block]
        planes = refs[-per_block:]
    def leave(channel):
        return pltpu.make_async_copy(visibility.at[channel], visibility_out.at[channel], left.at[channel])

    def arrange(channel, odd):
        power = jnp.zeros((in_dev, count), jnp.float32)
        for pair in range(blocks // 2):
            halves = []
            for other in (2 * pair + odd, 2 * pair + 1 - odd):
                wide = parts[other][channel, :, places[other] : places[other] + count].astype(jnp.float32)
                real_part, imag_part = wide[:in_dev], wide[in_dev:]
                power = power + (real_part * real_part + imag_part * imag_part)
                halves.append((real_part, imag_part))
            for plane, values in enumerate(zip(*halves)):
                planes[channel][plane, (me // 2) ^ pair] = jnp.concatenate(values, axis=0).astype(jnp.bfloat16)
        beam[channel : channel + 1, :] = jnp.sum(power, axis=0, keepdims=True) * (1.0 / inputs)

    for odd in range(2):

        @pl.when(me % 2 == odd)
        def _():
            for channel in range(per_block):
                arrange(channel, odd)
                both = planes[channel][...].reshape(2 * inputs, count)
                gram = lax.dot_general(both, both, (((1,), (1,)), ((), ())), preferred_element_type=jnp.float32)
                straight = (gram[:inputs, :inputs] + gram[inputs:, inputs:]) * (1.0 / SPECTRA)
                crossed = (gram[inputs:, :inputs] - gram[:inputs, inputs:]) * (1.0 / SPECTRA)
                if before is not None:
                    straight = before[channel, 0] + straight
                    crossed = before[channel, 1] + crossed
                visibility[channel, 0] = straight
                visibility[channel, 1] = crossed
                if chunks:
                    leave(channel).start()
    if chunks:
        copies += [leave(channel) for channel in range(per_block)]
        copies.append(pltpu.make_async_copy(beam, beam_out.at[:, pl.ds(start, count)], left.at[per_block]))
        copies[-1].start()
        for copy in copies:
            copy.wait()


def correlate(parts, start, count, blocks, before=None, chunks=(), beams=()):
    parts, places = zip(*parts)
    per_block, rows, _ = parts[0].shape
    in_dev = rows // 2
    inputs = in_dev * blocks
    visibility = (per_block, 2, inputs, inputs)
    space = pltpu.HBM if chunks else pltpu.VMEM
    staged = [
        pltpu.VMEM(visibility, jnp.float32),
        pltpu.VMEM((per_block, count), jnp.float32),
        pltpu.SemaphoreType.DMA((per_block + 1 + len(chunks),)),
    ]
    operands = [*parts, *([] if before is None else [before]), *beams]
    return pl.pallas_call(
        functools.partial(correlate_kernel, in_dev, blocks, places, start, count, chunks),
        in_specs=[pl.BlockSpec(memory_space=pltpu.VMEM)] * len(operands),
        out_specs=[pl.BlockSpec(memory_space=space)] * 2,
        scratch_shapes=(staged if chunks else [])
        + [pltpu.VMEM((2, blocks // 2, 2 * in_dev, count), jnp.bfloat16) for _ in range(per_block)],
        out_shape=[
            jax.ShapeDtypeStruct(visibility, jnp.float32),
            jax.ShapeDtypeStruct((per_block, SPECTRA if chunks else count), jnp.float32),
        ],
        compiler_params=pltpu.CompilerParams(vmem_limit_bytes=VMEM),
    )(*operands)


LEAD = 6
LEAD_FRAMES = 256
NEAR_ORDER = (4,5,1,2,6,3,7)
NEARS_AHEAD = (0, 1, 1, 1, 2, 1, 1, 0)
IN_FLIGHT = 5


def body(voltages, owner_block):
    in_dev = voltages.shape[0]
    blocks = lax.axis_size(AXES)
    half, per_block = blocks // 2, CHANS // blocks
    frames = voltages.reshape(in_dev, SPECTRA + TAPS - 1, LENGTH).transpose(1, 0, 2)
    inputs = (owner_block, frames, jnp.asarray(window_table()), jnp.asarray(dft_table()))
    far, near = tuple(range(half, blocks)), tuple(range(half))
    sent, taken = [], {}

    def send(target, block, other):
        if len(sent) >= IN_FLIGHT:
            before = sent[: 1 - IN_FLIGHT]
            block, *held = lax.optimization_barrier((block, *(taken[key] for key in before)))
            taken.update(zip(before, held))
        taken[target] = lax.ppermute(block, AXES, [(s, s ^ other) for s in range(blocks)])
        sent.append(target)

    first = [(other, 0, LEAD_FRAMES) for other in far[:LEAD]]
    made = make_spectra(inputs, LEAD_FRAMES, in_dev, blocks, first, True)
    send(first[0], made[0], half)
    last = [(other, LEAD_FRAMES, SPECTRA - LEAD_FRAMES) for other in far[:LEAD]]
    across = [(other, 0, SPECTRA) for other in far[LEAD:]]
    close = [(other, 0, SPECTRA) for other in near]
    targets = across + last + close
    ready = dict(zip(targets, make_spectra(made[1:], SPECTRA, in_dev, blocks, targets, False)))
    taken[close[0]] = ready[close[0]]
    distant, others = list(across + last), [close[step] for step in NEAR_ORDER if step < half]
    others += [target for target in close[1:] if target not in others]
    order = []
    for near_before in NEARS_AHEAD:
        order += others[:near_before] + distant[:1]
        others, distant = others[near_before:], distant[1:]
    for target in order + others + distant:
        block, step = ready[target], target[0]
        if 0 < step < LEAD:
            handed = taken[first[0]][step * per_block : (step + 1) * per_block]
            block = jnp.concatenate([block, handed], axis=2)
        send(target, block, step)

    places = {first[0]: (taken[first[0]], 0)}
    places.update((first[step], (taken[close[step]], SPECTRA)) for step in range(1, LEAD))
    early = [(taken[target], 0) for target in close] + [places[target] for target in first]
    late = [(taken[target], LEAD_FRAMES) for target in close] + [(taken[target], 0) for target in last]
    visibility, beam = correlate(early + [(taken[target], 0) for target in across], 0, LEAD_FRAMES, blocks)
    visibility, beam = correlate(
        late + [(taken[target], LEAD_FRAMES) for target in across], LEAD_FRAMES, SPECTRA - LEAD_FRAMES, blocks,
        visibility, ((0, LEAD_FRAMES),), (beam,),
    )
    return (visibility[None], beam[None])


def solution(mesh):
    in_specs = (P(("groups", "row", "col"), None), P())
    out_specs = (
        P(("groups", "row", "col"), None, None, None, None),
        P(("groups", "row", "col"), None, None),
    )
    return jax.shard_map(body, mesh=mesh, in_specs=in_specs, out_specs=out_specs, check_vma=False)
```

```python
import functools
import math

import jax
import jax.numpy as jnp
import numpy as np
from jax import lax
from jax.experimental import pallas as pl
from jax.experimental.pallas import tpu as pltpu
from jax.sharding import PartitionSpec as P

CHANS = 128
TAPS = 8
SPECTRA = 1024
LENGTH = 2 * CHANS
AXES = ("row", "col")
LANES = 128
FRAME_GROUP = 32
FIRST_TILE = 128
TILE = 256
VMEM = 40 * 1024 * 1024


def window_table():
    total = TAPS * LENGTH
    offsets = np.arange(total, dtype=np.float64)
    profile = np.sinc((offsets - total / 2 + 0.5) / LENGTH) * (
        0.5 - 0.5 * np.cos(2 * math.pi * (offsets + 0.5) / total)
    )
    profile = profile * np.sqrt(LENGTH / np.sum(profile * profile))
    return profile.reshape(TAPS, LENGTH).astype(np.float32)


def dft_table():
    times = np.arange(LENGTH)
    freqs = np.arange(CHANS)
    phase = 2 * math.pi * ((freqs[:, None] * times[None, :]) % LENGTH) / LENGTH
    table = np.concatenate([np.cos(phase), -np.sin(phase)], 0) / math.sqrt(LENGTH)
    return table.astype(np.float32).astype(jnp.bfloat16).astype(np.float32)


def spectra_tile(start, in_dev, targets, base_of, outs, frames, window, fourier, filtered, spectra):
    tile = filtered.shape[1] // in_dev

    @pl.loop(0, tile // FRAME_GROUP)
    def _(group):
        first = start + group * FRAME_GROUP
        for half in range(LENGTH // LANES):
            cols = slice(half * LANES, (half + 1) * LANES)
            held = frames[pl.ds(first, FRAME_GROUP + TAPS - 1), :, cols].astype(jnp.float32)
            total = window[0:1, cols] * held[0:FRAME_GROUP]
            for tap in range(1, TAPS):
                total = total + window[tap : tap + 1, cols] * held[tap : tap + FRAME_GROUP]
            filtered[half, pl.ds(group * FRAME_GROUP * in_dev, FRAME_GROUP * in_dev), :] = total.reshape(
                FRAME_GROUP * in_dev, LANES
            )

    table = fourier()
    height = table.shape[0]
    for i in range(in_dev):
        rows = jnp.concatenate(
            [filtered[half, pl.ds(i, tile, stride=in_dev), :] for half in range(LENGTH // LANES)], axis=1
        ).astype(jnp.bfloat16)
        product = lax.dot_general(
            table, rows, (((1,), (1,)), ((), ())), preferred_element_type=jnp.float32
        )
        for part in range(tile // LANES):
            spectra[part, pl.ds(i * height, height), :] = product[:, part * LANES : (part + 1) * LANES]
    for (other, low, width), out in zip(targets, outs):
        if not low <= start < low + width:
            continue
        bases = base_of(other)
        offset = start - low
        for channel in range(out.shape[0]):
            for part in range(tile // LANES):
                pair = [
                    spectra[part, pl.ds(base + channel, in_dev, stride=height), :]
                    for base in bases
                ]
                out[channel, :, offset + part * LANES : offset + (part + 1) * LANES] = jnp.concatenate(
                    pair, axis=0
                ).astype(jnp.bfloat16)


def first_spectra_kernel(count, in_dev, blocks, targets, *refs):
    owner_in, frames_in, window_in, fourier_in = refs[:4]
    per_block = CHANS // blocks
    outs = [refs[4].at[pl.ds(index * per_block, per_block)] for index in range(len(targets))]
    frames, window, fourier, owner_held, filtered, spectra, owner, arrived = refs[5:]
    me = lax.axis_index(AXES)
    aligned, order = per_block % 8 == 0, [other for other, _, _ in targets]
    needed, total = count + TAPS - 1, SPECTRA + TAPS - 1
    window_copy = pltpu.make_async_copy(window_in, window, arrived.at[0])
    fourier_copy = pltpu.make_async_copy(fourier_in, fourier, arrived.at[1])
    owner_copy = pltpu.make_async_copy(owner_in, owner, arrived.at[2])
    held_copy = pltpu.make_async_copy(owner_in, owner_held, arrived.at[3])
    edges = sorted({0, FIRST_TILE + TAPS - 1, needed, total})
    frame_copies = [
        pltpu.make_async_copy(frames_in.at[pl.ds(low, high - low)], frames.at[pl.ds(low, high - low)], arrived.at[4 + index])
        for index, (low, high) in enumerate(zip(edges, edges[1:]))
    ]
    copies = [window_copy, frame_copies[0], fourier_copy, owner_copy, *frame_copies[1:], held_copy]
    for copy in copies:
        copy.start()
    window_copy.wait()
    for start in range(0, count, FIRST_TILE):
        if start < 2 * FIRST_TILE:
            frame_copies[start // FIRST_TILE].wait()

        def needed_rows():
            if start == 0:
                fourier_copy.wait()
                owner_copy.wait()
            if not aligned:
                return fourier[...].astype(jnp.bfloat16)
            return jnp.concatenate(
                [
                    fourier[pl.ds(pl.multiple_of(owner[me ^ other] * per_block + plane * CHANS, per_block), per_block), :]
                    for other, _, _ in targets
                    for plane in range(2)
                ],
                axis=0,
            ).astype(jnp.bfloat16)

        def base_of(other):
            if aligned:
                index = order.index(other)
                return 2 * index * per_block, (2 * index + 1) * per_block
            return tuple(owner[me ^ other] * per_block + plane * CHANS for plane in range(2))

        spectra_tile(start, in_dev, targets, base_of, outs, frames, window, needed_rows, filtered, spectra)
    held_copy.wait()
    frame_copies[-1].wait()


def spectra_kernel(count, in_dev, blocks, targets, *refs):
    frames, window, fourier, owner_held = refs[:4]
    outs = refs[4 : 4 + len(targets)]
    filtered, spectra, owner, arrived = refs[4 + len(targets) :]
    me = lax.axis_index(AXES)
    owner_copy = pltpu.make_async_copy(owner_held, owner, arrived.at[0])
    owner_copy.start()
    owner_copy.wait()

    def base_of(other):
        return tuple(owner[me ^ other] * (CHANS // blocks) + plane * CHANS for plane in range(2))

    for start in range(0, count, TILE):
        spectra_tile(
            start, in_dev, targets, base_of, outs, frames, window, lambda: fourier[...].astype(jnp.bfloat16), filtered, spectra
        )


def make_spectra(inputs, count, in_dev, blocks, targets, first):
    per_block = CHANS // blocks
    rows = 2 * in_dev
    vmem, hbm = pl.BlockSpec(memory_space=pltpu.VMEM), pl.BlockSpec(memory_space=pltpu.HBM)
    out_shape = [jax.ShapeDtypeStruct((per_block, rows, width), jnp.bfloat16) for _, _, width in targets]
    tile = FIRST_TILE if first else TILE
    scratch = [
        pltpu.VMEM((LENGTH // LANES, tile * in_dev, LANES), jnp.float32),
        pltpu.VMEM((tile // LANES, in_dev * 2 * CHANS, LANES), jnp.float32),
        pltpu.SMEM((blocks,), jnp.int32),
    ]
    if first:
        owner_block, frames, window, fourier = inputs
        kernel = functools.partial(first_spectra_kernel, count, in_dev, blocks, targets)
        out_shape = [jax.ShapeDtypeStruct((len(targets) * per_block, rows, count), jnp.bfloat16)]
        out_shape += [jax.ShapeDtypeStruct(x.shape, x.dtype) for x in (frames, window, fourier, owner_block)]
        in_specs = [hbm] * 4
        inputs = [pltpu.with_memory_space_constraint(x, pltpu.HBM) for x in inputs]
        scratch.append(pltpu.SemaphoreType.DMA((8,)))
    else:
        kernel = functools.partial(spectra_kernel, count, in_dev, blocks, targets)
        in_specs = [vmem] * 4
        scratch.append(pltpu.SemaphoreType.DMA((1,)))
    return pl.pallas_call(
        kernel,
        in_specs=in_specs,
        out_specs=[vmem] * len(out_shape),
        out_shape=out_shape,
        scratch_shapes=scratch,
        compiler_params=pltpu.CompilerParams(vmem_limit_bytes=VMEM),
    )(*inputs)


def correlate_kernel(in_dev, blocks, places, start, count, chunks, *refs):
    parts = refs[:blocks]
    per_block = parts[0].shape[0]
    inputs = in_dev * blocks
    me = lax.axis_index(AXES)
    if chunks:
        before, beams = refs[blocks], refs[blocks + 1 : blocks + 1 + len(chunks)]
        visibility_out, beam_out, visibility, beam, left = refs[blocks + 1 + len(chunks) : blocks + 6 + len(chunks)]
        planes = refs[blocks + 6 + len(chunks) :]
        copies = [
            pltpu.make_async_copy(held, beam_out.at[:, pl.ds(first, size)], left.at[per_block + 1 + index])
            for index, ((first, size), held) in enumerate(zip(chunks, beams))
        ]
        for copy in copies:
            copy.start()
    else:
        before = refs[blocks] if len(refs) == blocks + 3 + per_block else None
        visibility, beam = refs[-per_block - 2 : -per_block]
        planes = refs[-per_block:]
    def leave(channel):
        return pltpu.make_async_copy(visibility.at[channel], visibility_out.at[channel], left.at[channel])

    def arrange(channel, odd):
        power = jnp.zeros((in_dev, count), jnp.float32)
        for pair in range(blocks // 2):
            halves = []
            for other in (2 * pair + odd, 2 * pair + 1 - odd):
                wide = parts[other][channel, :, places[other] : places[other] + count].astype(jnp.float32)
                real_part, imag_part = wide[:in_dev], wide[in_dev:]
                power = power + (real_part * real_part + imag_part * imag_part)
                halves.append((real_part, imag_part))
            for plane, values in enumerate(zip(*halves)):
                planes[channel][plane, (me // 2) ^ pair] = jnp.concatenate(values, axis=0).astype(jnp.bfloat16)
        beam[channel : channel + 1, :] = jnp.sum(power, axis=0, keepdims=True) * (1.0 / inputs)

    for odd in range(2):

        @pl.when(me % 2 == odd)
        def _():
            for channel in range(per_block):
                arrange(channel, odd)
                both = planes[channel][...].reshape(2 * inputs, count)
                gram = lax.dot_general(both, both, (((1,), (1,)), ((), ())), preferred_element_type=jnp.float32)
                straight = (gram[:inputs, :inputs] + gram[inputs:, inputs:]) * (1.0 / SPECTRA)
                crossed = (gram[inputs:, :inputs] - gram[:inputs, inputs:]) * (1.0 / SPECTRA)
                if before is not None:
                    straight = before[channel, 0] + straight
                    crossed = before[channel, 1] + crossed
                visibility[channel, 0] = straight
                visibility[channel, 1] = crossed
                if chunks:
                    leave(channel).start()
    if chunks:
        copies += [leave(channel) for channel in range(per_block)]
        copies.append(pltpu.make_async_copy(beam, beam_out.at[:, pl.ds(start, count)], left.at[per_block]))
        copies[-1].start()
        for copy in copies:
            copy.wait()


def correlate(parts, start, count, blocks, before=None, chunks=(), beams=()):
    parts, places = zip(*parts)
    per_block, rows, _ = parts[0].shape
    in_dev = rows // 2
    inputs = in_dev * blocks
    visibility = (per_block, 2, inputs, inputs)
    space = pltpu.HBM if chunks else pltpu.VMEM
    staged = [
        pltpu.VMEM(visibility, jnp.float32),
        pltpu.VMEM((per_block, count), jnp.float32),
        pltpu.SemaphoreType.DMA((per_block + 1 + len(chunks),)),
    ]
    operands = [*parts, *([] if before is None else [before]), *beams]
    return pl.pallas_call(
        functools.partial(correlate_kernel, in_dev, blocks, places, start, count, chunks),
        in_specs=[pl.BlockSpec(memory_space=pltpu.VMEM)] * len(operands),
        out_specs=[pl.BlockSpec(memory_space=space)] * 2,
        scratch_shapes=(staged if chunks else [])
        + [pltpu.VMEM((2, blocks // 2, 2 * in_dev, count), jnp.bfloat16) for _ in range(per_block)],
        out_shape=[
            jax.ShapeDtypeStruct(visibility, jnp.float32),
            jax.ShapeDtypeStruct((per_block, SPECTRA if chunks else count), jnp.float32),
        ],
        compiler_params=pltpu.CompilerParams(vmem_limit_bytes=VMEM),
    )(*operands)


LEAD = 6
LEAD_FRAMES = 256
NEAR_ORDER = (4,5,1,2,6,3,7)
NEARS_AHEAD = (0, 1, 1, 1, 2, 1, 1, 0)
IN_FLIGHT = 5


def body(voltages, owner_block):
    in_dev = voltages.shape[0]
    blocks = lax.axis_size(AXES)
    half, per_block = blocks // 2, CHANS // blocks
    frames = voltages.reshape(in_dev, SPECTRA + TAPS - 1, LENGTH).transpose(1, 0, 2)
    inputs = (owner_block, frames, jnp.asarray(window_table()), jnp.asarray(dft_table()))
    far, near = tuple(range(half, blocks)), tuple(range(half))
    sent, taken = [], {}

    def send(target, block, other):
        if len(sent) >= IN_FLIGHT:
            before = sent[: 1 - IN_FLIGHT]
            block, *held = lax.optimization_barrier((block, *(taken[key] for key in before)))
            taken.update(zip(before, held))
        taken[target] = lax.ppermute(block, AXES, [(s, s ^ other) for s in range(blocks)])
        sent.append(target)

    first = [(other, 0, LEAD_FRAMES) for other in far[:LEAD]]
    made = make_spectra(inputs, LEAD_FRAMES, in_dev, blocks, first, True)
    send(first[0], made[0], half)
    last = [(other, LEAD_FRAMES, SPECTRA - LEAD_FRAMES) for other in far[:LEAD]]
    across = [(other, 0, SPECTRA) for other in far[LEAD:]]
    close = [(other, 0, SPECTRA) for other in near]
    targets = across + last + close
    ready = dict(zip(targets, make_spectra(made[1:], SPECTRA, in_dev, blocks, targets, False)))
    taken[close[0]] = ready[close[0]]
    distant, others = list(across[::-1] + last), [close[step] for step in NEAR_ORDER if step < half]
    others += [target for target in close[1:] if target not in others]
    order = []
    for near_before in NEARS_AHEAD:
        order += others[:near_before] + distant[:1]
        others, distant = others[near_before:], distant[1:]
    for target in order + others + distant:
        block, step = ready[target], target[0]
        if 0 < step < LEAD:
            handed = taken[first[0]][step * per_block : (step + 1) * per_block]
            block = jnp.concatenate([block, handed], axis=2)
        send(target, block, step)

    places = {first[0]: (taken[first[0]], 0)}
    places.update((first[step], (taken[close[step]], SPECTRA)) for step in range(1, LEAD))
    early = [(taken[target], 0) for target in close] + [places[target] for target in first]
    late = [(taken[target], LEAD_FRAMES) for target in close] + [(taken[target], 0) for target in last]
    visibility, beam = correlate(early + [(taken[target], 0) for target in across], 0, LEAD_FRAMES, blocks)
    visibility, beam = correlate(
        late + [(taken[target], LEAD_FRAMES) for target in across], LEAD_FRAMES, SPECTRA - LEAD_FRAMES, blocks,
        visibility, ((0, LEAD_FRAMES),), (beam,),
    )
    return (visibility[None], beam[None])


def solution(mesh):
    in_specs = (P(("groups", "row", "col"), None), P())
    out_specs = (
        P(("groups", "row", "col"), None, None, None, None),
        P(("groups", "row", "col"), None, None),
    )
    return jax.shard_map(body, mesh=mesh, in_specs=in_specs, out_specs=out_specs, check_vma=False)
```
